256 devices in a mesh: dp: 8 (over y, core), expert: 32 (over x, z).
Axes of the slice: x: 4, y: 4, z: 8, core: 2. Of those that a mesh axis runs over, the one named last changes fastest.
Arguments:
- tokens_in: bfloat16 [32, 4096, 3584], P('expert', 'dp'), may hold values from -6 to 6
- grad_out: bfloat16 [32, 4096, 1024], P('expert', 'dp'), may hold values from -0.3984375 to 0.3984375
- token_counts: int32 [32, 8], P('expert', 'dp'), may hold values from 1 to 512, as said below
- new_owner: int32 [32], replicated, may hold values from 0 to 31, as said below
- master: float32 [32, 3584, 1024], P('expert', 'dp'), may hold values from -0.3 to 0.3
- moment_one: bfloat16 [32, 3584, 1024], P('expert', 'dp'), may hold values from -6 to 6
- moment_two: bfloat16 [32, 3584, 1024], P('expert', 'dp'), may hold values from 0.099609375 to 10
Outputs:
- master_out: float32 [32, 3584, 1024], P('expert', 'dp')
- moment_one_out: bfloat16 [32, 3584, 1024], P('expert', 'dp')
- moment_two_out: bfloat16 [32, 3584, 1024], P('expert', 'dp')
- weight_out: bfloat16 [32, 3584, 1024], P('expert', 'dp')
The draws below stay inside these ranges and needn't reach their ends.
Inputs may be any that keep to these rules, and one draw needn't show every extreme that they name: `token_counts`: for each replica some expert has exactly 512 live slots. `new_owner`: a permutation of the owners in which exactly 3 entries differ from their index.
All inputs are finite; a program needn't handle non-finite values.
Results may differ from the reference program's by a relative error of at most 0.013.
Values may be sent and summed in bfloat16 or wider, within the bound.
No kernel may reach another device: no remote copies, remote signals or barrier semaphores. Data moves between devices by JAX's collectives and lax.ppermute only.
A program may use at most 128 MiB of HBM per device.

```python
import math
import jax
import jax.numpy as jnp
from jax import lax

D = 3584
FFW = 1024
CAP = 512
MOVES = 3
STEP = 10
EXPERTS = 32
ROWS = 4096
N_DP = 8


def draw_token_counts(key, part):
    key = jax.random.fold_in(key, 11)
    heat_key, fill_key, peak_key = jax.random.split(key, 3)
    heat_level = jax.random.randint(heat_key, (EXPERTS, 1), 1, 5)
    base_count = jax.random.randint(fill_key, (EXPERTS, N_DP), 1, CAP // 2 + 1)
    tallies = jnp.minimum(base_count * heat_level, CAP)
    peak_expert = jax.random.randint(peak_key, (1, N_DP), 0, EXPERTS)
    expert_index = jnp.arange(EXPERTS, dtype=jnp.int32)[:, None]
    return jnp.where(expert_index == peak_expert, CAP, tallies).astype(jnp.int32)


def draw_new_owner(key, part):
    key = jax.random.fold_in(key, 7)
    shuffled = jax.random.permutation(key, EXPERTS)
    chosen = shuffled[:MOVES]
    target = jnp.roll(chosen, 1)
    owner_index = jnp.arange(EXPERTS, dtype=jnp.int32)
    return owner_index.at[chosen].set(target.astype(jnp.int32)).astype(jnp.int32)


def block_levels(key, extent, cuts, least, largest):
    def one(position, parts):
        heights = jax.random.uniform(jax.random.fold_in(jax.random.fold_in(key, 6), position), (parts,), jnp.float32, least / len(cuts), largest / len(cuts))
        return jnp.repeat(jnp.exp(heights), extent[position] // parts).reshape((-1,) + (1,) * (len(extent) - position - 1))

    factor_of = one(*cuts[0])
    for cut in cuts[1:]:
        factor_of = factor_of * one(*cut)
    return factor_of


def scatter_about(rng, extent, deviation, bound, pieces=(), held_as=jnp.bfloat16):
    result = jax.random.normal(rng, extent, jnp.float32) * deviation
    if len(pieces) > 0:
        result = block_levels(rng, extent, pieces, -0.22, 0.18) * result
    return jnp.clip(result, min=-bound, max=bound).astype(held_as)


def setup_inputs(seed: int = 0) -> dict:
    arg_keys = jax.random.split(jax.random.key(seed), 8)
    tokens_in = scatter_about(arg_keys[0], (EXPERTS, ROWS, D), 1.0, 6.0, ((0, 32), (1, 8)))
    grad_out = scatter_about(arg_keys[1], (EXPERTS, ROWS, FFW), 0.0625, 0.3984375, ((0, 32), (1, 8)))
    token_counts = draw_token_counts(jax.random.fold_in(arg_keys[7], 71), 0)
    new_owner = draw_new_owner(jax.random.fold_in(arg_keys[7], 71), 0)
    master = scatter_about(arg_keys[4], (EXPERTS, D, FFW), 0.05, 0.3, ((0, 32), (1, 8)), jnp.float32)
    moment_one = scatter_about(arg_keys[5], (EXPERTS, D, FFW), 1.0, 6.0, ((0, 32), (1, 8)))
    moment_two = jnp.clip(jnp.exp(math.log(10.0) - 4.609084 * jax.random.uniform(arg_keys[6], (EXPERTS, D, FFW), jnp.float32) ** block_levels(arg_keys[6], (EXPERTS, D, FFW), ((0, 32), (1, 8)), -0.2, 0.2)), 0.099609375, 10.0).astype(jnp.bfloat16)
    return dict(tokens_in=tokens_in, grad_out=grad_out, token_counts=token_counts, new_owner=new_owner, master=master, moment_one=moment_one, moment_two=moment_two)


beta_one = 0.9
beta_two = 0.95
learn_rate = 0.001
decay_rate = 0.1
adam_eps = 1e-08

def adamw_step(master, moment_one, moment_two, gradient):
    moment_new = beta_one * moment_one.astype(jnp.float32) + (1.0 - beta_one) * gradient
    second_new = beta_two * moment_two.astype(jnp.float32) + (1.0 - beta_two) * gradient * gradient
    scaled_one = moment_new / (1.0 - beta_one ** STEP)
    scaled_two = second_new / (1.0 - beta_two ** STEP)
    updated = master - learn_rate * (scaled_one / (jnp.sqrt(scaled_two) + adam_eps) + decay_rate * master)
    return (updated, moment_new.astype(jnp.bfloat16), second_new.astype(jnp.bfloat16))

def one_expert(packed):
    features, cotangent, counts, master, moment_one, moment_two = packed
    live_rows = jnp.arange(CAP, dtype=jnp.int32)[None, :] < counts[:, None]
    masked = jnp.where(live_rows[:, :, None], cotangent, jnp.zeros_like(cotangent))
    partial_value = jnp.einsum('itd,itf->idf', features.astype(jnp.float32), masked.astype(jnp.float32))
    rounded = lax.optimization_barrier(partial_value.astype(jnp.bfloat16))
    gradient = lax.optimization_barrier(jnp.sum(rounded.astype(jnp.float32), axis=0))
    return adamw_step(master, moment_one, moment_two, gradient)

def reference(tokens_in, grad_out, token_counts, new_owner, master, moment_one, moment_two):
    features = tokens_in.reshape(EXPERTS, N_DP, CAP, D)
    cotangent = grad_out.reshape(EXPERTS, N_DP, CAP, FFW)
    updated, moment_new, second_new = lax.map(one_expert, (features, cotangent, token_counts, master, moment_one, moment_two))
    new_slots = new_owner.astype(jnp.int32)
    master_out = jnp.zeros_like(updated).at[new_slots].set(updated)
    moment_one_out = jnp.zeros_like(moment_new).at[new_slots].set(moment_new)
    moment_two_out = jnp.zeros_like(second_new).at[new_slots].set(second_new)
    weight_out = master_out.astype(jnp.bfloat16)
    return (master_out, moment_one_out, moment_two_out, weight_out)
```

```python
import itertools

import jax
import jax.numpy as jnp
from jax import lax
from jax.sharding import Mesh, PartitionSpec as P

STEP = 10
NX = 4
NZ = 8

beta_one = 0.9
beta_two = 0.95
learn_rate = 0.001
decay_rate = 0.1
adam_eps = 1e-08


def adamw_step(master, moment_one, moment_two, gradient):
    moment_new = beta_one * moment_one.astype(jnp.float32) + (1.0 - beta_one) * gradient
    second_new = beta_two * moment_two.astype(jnp.float32) + (1.0 - beta_two) * gradient * gradient
    scaled_one = moment_new / (1.0 - beta_one**STEP)
    scaled_two = second_new / (1.0 - beta_two**STEP)
    updated = master - learn_rate * (
        scaled_one / (jnp.sqrt(scaled_two) + adam_eps) + decay_rate * master
    )
    return (updated, moment_new.astype(jnp.bfloat16), second_new.astype(jnp.bfloat16))


def row_moves(n):
    found = [{}]
    for a, b in itertools.combinations(range(n), 2):
        found.append({a: b, b: a})
    for a, b, c in itertools.combinations(range(n), 3):
        found.append({a: b, b: c, c: a})
        found.append({a: c, c: b, b: a})
    return found


Z_MOVES = row_moves(NZ)


def move_code(move):
    return sum((to - at) * NZ**at for at, to in move.items())


class Plan:
    def __init__(self, new_owner):
        owners = jnp.arange(NX * NZ, dtype=jnp.int32)
        at_z, to_z = owners % NZ, new_owner % NZ
        code = jnp.sum((to_z - at_z) * NZ**at_z)
        codes = jnp.array([move_code(m) for m in Z_MOVES], jnp.int32)
        self.branch = jnp.sum(jnp.where(codes == code, jnp.arange(len(Z_MOVES), dtype=jnp.int32), 0))
        my_x, my_z = lax.axis_index("x"), lax.axis_index("z")
        self.leaver = jnp.sum(jnp.where((at_z == my_z) & (to_z != my_z), owners // NZ, 0))
        source = jnp.sum(
            jnp.where(new_owner[None, :] == owners[:, None], owners[None, :], 0), axis=1
        )
        mine = lax.dynamic_slice(source.reshape(NX, NZ), (0, my_z), (NX, 1))[:, 0]
        self.source_x = mine // NZ
        self.source_here = (mine % NZ) == my_z
        me = my_x * NZ + my_z
        self.moved = lax.dynamic_index_in_dim(source, me, keepdims=False) != me


def relocate(pieces, plan):
    spread = lax.all_to_all(pieces, "x", split_axis=0, concat_axis=0, tiled=True)
    leaving = lax.dynamic_index_in_dim(spread, plan.leaver, 0, keepdims=False)

    def branch(move):
        if not move:
            return lambda a: a
        return lambda a: lax.ppermute(a, "z", sorted(move.items()))

    arrived = lax.switch(plan.branch, [branch(m) for m in Z_MOVES], leaving)
    picked = jnp.stack(
        [
            jnp.where(
                plan.source_here[i],
                lax.dynamic_index_in_dim(spread, plan.source_x[i], 0, keepdims=False),
                arrived,
            )
            for i in range(NX)
        ]
    )
    return lax.all_to_all(picked, "x", split_axis=0, concat_axis=0, tiled=True)


def local(tokens_in, grad_out, token_counts, new_owner, master, moment_one, moment_two):
    features = tokens_in[0]
    plan = Plan(new_owner)
    live_count = token_counts[0, 0]
    live_rows = jnp.arange(features.shape[0], dtype=jnp.int32) < live_count
    masked = jnp.where(live_rows[:, None], grad_out[0], jnp.zeros_like(grad_out[0]))
    gradient = lax.psum_scatter(
        jnp.einsum("td,tf->df", features, masked, preferred_element_type=jnp.float32).astype(
            jnp.bfloat16
        ),
        ("y", "core"),
        scatter_dimension=0,
        tiled=True,
    )
    rows, cols = gradient.shape
    part = rows // NX
    own = (master[0], moment_one[0], moment_two[0])
    state = jnp.concatenate(
        [a.astype(jnp.bfloat16).reshape(NX, part, cols) for a in own], axis=1
    )
    state = relocate(state, plan)
    came = [state[:, k * part : (k + 1) * part].reshape(rows, cols) for k in range(3)]
    new_gradient = relocate(gradient.reshape(NX, part, cols), plan).reshape(rows, cols)
    old = [jnp.where(plan.moved, b.astype(a.dtype), a) for a, b in zip(own, came)]
    new_master, new_one, new_two = adamw_step(*old, new_gradient.astype(jnp.float32))
    return (new_master[None], new_one[None], new_two[None], new_master.astype(jnp.bfloat16)[None])


def solution(mesh):
    n_dp = mesh.devices.shape[0]
    fine = Mesh(mesh.devices.reshape(n_dp // 2, 2, NX, NZ), ("y", "core", "x", "z"))
    dp, expert = ("y", "core"), ("x", "z")
    whole = P(expert, dp, None)
    return jax.shard_map(
        local,
        mesh=fine,
        in_specs=(whole, whole, P(expert, dp), P(), whole, whole, whole),
        out_specs=(whole, whole, whole, whole),
        check_vma=False,
    )
```

```python
import functools

import jax
import jax.numpy as jnp
from jax import lax
from jax.experimental import pallas as pl
from jax.experimental.pallas import tpu as pltpu
from jax.sharding import Mesh, PartitionSpec as P

STEP = 10
NX = 4
NZ = 8
N = NX * NZ
UP = NZ // 2
DOWN = NZ - 1 - UP

beta_one = 0.9
beta_two = 0.95
learn_rate = 0.001
decay_rate = 0.1
adam_eps = 1e-08

BF = jnp.bfloat16
F32 = jnp.float32
ANY = pl.BlockSpec(memory_space=pl.ANY)


def params(mib):
    return pltpu.CompilerParams(vmem_limit_bytes=mib * 2**20)


def prefetch(grid, in_specs, out_specs, scratch=()):
    return pltpu.PrefetchScalarGridSpec(
        num_scalar_prefetch=1,
        grid=grid,
        in_specs=in_specs,
        out_specs=out_specs,
        scratch_shapes=scratch,
    )


def partial_kernel(count, tokens, grads, *refs):
    out, masked, turned = refs[-3:]

    @pl.when(pl.program_id(0) == 0)
    def _():
        live = lax.broadcasted_iota(jnp.int32, grads.shape, 0) < count[0]
        masked[...] = jnp.where(live, grads[...].astype(F32), 0.0).astype(BF)

    turned[...] = tokens[...].T
    out[...] = jnp.dot(turned[...], masked[...], preferred_element_type=F32).astype(BF)


def partial_gradient(count, tokens, grads, after):
    cap, feats = tokens.shape
    ffw = grads.shape[1]
    step = feats // 7
    return pl.pallas_call(
        partial_kernel,
        out_shape=jax.ShapeDtypeStruct((feats, ffw), BF),
        grid_spec=prefetch(
            (feats // step,),
            [
                pl.BlockSpec((cap, step), lambda i, count: (0, i)),
                pl.BlockSpec((cap, ffw), lambda i, count: (0, 0)),
            ]
            + [ANY] * len(after),
            pl.BlockSpec((step, ffw), lambda i, count: (i, 0)),
            [pltpu.VMEM((cap, ffw), BF), pltpu.VMEM((step, cap), BF)],
        ),
        compiler_params=params(40),
    )(count, tokens, grads, *after)


MY_X, MOVED, LEAVER, GO_UP, GO_DOWN, PICK = 0, 1, 2, 3, 4, 5


def plan_kernel(place, new_owner, out):
    my_x, my_z = place[0], place[1]
    me = my_x * NZ + my_z
    leaver, moved, up, down = jnp.int32(0), jnp.int32(0), jnp.int32(0), jnp.int32(0)
    for e in range(N):
        to = new_owner[e]
        x, z = e // NZ, e % NZ
        away = (to + NZ - z) % NZ
        mine = (my_z == z) & (away != 0)
        dist = (x + NX - my_x) % NX
        leaver += jnp.where(mine, dist, 0)
        up += jnp.where(mine & (away <= UP), 1, 0)
        down += jnp.where(mine & (away > UP), 1, 0)
        moved += jnp.where((to == me) & (to != e), 1, 0)

        @pl.when(to % NZ == my_z)
        def _():
            along = jnp.where(away <= UP, NX - 1 + away, NX + UP + NZ - 1 - away)
            out[PICK + (to // NZ + NX - my_x) % NX] = jnp.where(away == 0, dist, along)

    out[MY_X] = my_x
    out[MOVED] = moved
    out[LEAVER] = leaver
    out[GO_UP] = up
    out[GO_DOWN] = down


def make_plan(place, new_owner):
    smem = pl.BlockSpec(memory_space=pltpu.SMEM)
    return pl.pallas_call(
        plan_kernel,
        out_shape=jax.ShapeDtypeStruct((PICK + NX,), jnp.int32),
        in_specs=[smem] * 2,
        out_specs=smem,
    )(place, new_owner)


def pack_kernel(n, place, *refs):
    own, outs = refs[:n], refs[-n * NX :]
    for d in range(NX):

        @pl.when(pl.program_id(0) == d)
        def _():
            for u in range(n):
                outs[u * NX + d][...] = own[u][...].astype(BF)


def pack(place, own, after=()):
    rows, width = own[0].shape
    part, n = rows // NX, len(own)
    spec = pl.BlockSpec((part, width), lambda i, place: ((place[0] + i) % NX, 0))
    out_spec = pl.BlockSpec((part, width), lambda i, place: (0, 0))
    made = pl.pallas_call(
        functools.partial(pack_kernel, n),
        out_shape=[jax.ShapeDtypeStruct((part, width), BF)] * (NX * n),
        grid_spec=prefetch((NX,), [spec] * n + [ANY] * len(after), [out_spec] * (NX * n)),
        compiler_params=params(24),
    )(place, *own, *after)
    return [made[u * NX : (u + 1) * NX] for u in range(n)]


def pick_kernel(n, which, plan, *refs):
    cases, outs, sems = refs[:n], refs[n:-1], refs[-1]
    for k, (out, chosen) in enumerate(zip(outs, which(plan))):
        for c in range(n):

            @pl.when(chosen == c)
            def _():
                pltpu.make_async_copy(cases[c], out, sems.at[k]).start()

    for k, out in enumerate(outs):
        pltpu.make_async_copy(cases[0], out, sems.at[k]).wait()


def pick(plan, which, n_out, cases):
    shape = cases[0].shape
    return pl.pallas_call(
        functools.partial(pick_kernel, len(cases), which),
        out_shape=[jax.ShapeDtypeStruct(shape, BF)] * n_out,
        grid_spec=prefetch(
            (1,),
            [ANY] * len(cases),
            [pl.BlockSpec(shape, lambda i, plan: (0, 0))] * n_out,
            [pltpu.SemaphoreType.DMA((n_out,))],
        ),
        compiler_params=params(16),
    )(plan, *cases)


def ring(a, axis, size, by):
    return lax.ppermute(a, axis, [(i, (i + by) % size) for i in range(size)])


def swap_x(pieces):
    came = list(pieces)
    for d in (1, 3, 2):
        came[(-d) % NX] = ring(pieces[d], "x", NX, d)
    return came


def along_z(plan, spreads):
    n = len(spreads)
    (first,) = pick(plan, lambda plan: [plan[LEAVER]], 1, spreads[0])
    ups, downs = [ring(first, "z", NZ, 1)], [ring(first, "z", NZ, -1)]

    def own_or_passed(plan):
        return [
            jnp.where(plan[GO_UP] != 0, plan[LEAVER], NX),
            jnp.where(plan[GO_DOWN] != 0, plan[LEAVER], NX + 1),
        ]

    for t in range(1, n):
        up, down = pick(plan, own_or_passed, 2, [*spreads[t], ups[-1], downs[-1]])
        ups.append(ring(up, "z", NZ, 1))
        downs.append(ring(down, "z", NZ, -1))
    while len(ups) < n + UP - 1:
        ups.append(ring(ups[-1], "z", NZ, 1))
    while len(downs) < n + DOWN - 1:
        downs.append(ring(downs[-1], "z", NZ, -1))
    return [ups[j : j + UP] + downs[j : j + DOWN] for j in range(n)]


def relocate(plan, packed):
    spreads = [swap_x(pieces) for pieces in packed]

    def delivered(plan):
        return [plan[PICK + d] for d in range(NX)]

    return [
        swap_x(pick(plan, delivered, NX, [*spread, *came]))
        for spread, came in zip(spreads, along_z(plan, spreads))
    ]


def adam_kernel(plan, own_master, own_one, own_two, *refs):
    grads, came = refs[:NX], refs[NX : 4 * NX]
    out_master, out_one, out_two, out_weight = refs[4 * NX : 4 * NX + 4]
    grad, held, grad_sems, sems = refs[4 * NX + 4 :]
    step = pl.program_id(0)
    here = plan[MOVED] != 0

    def grad_copy(d):
        return pltpu.make_async_copy(grads[d], grad.at[d], grad_sems.at[d])

    def copies(d):
        return [
            pltpu.make_async_copy(came[u * NX + d], held.at[u, d], sems.at[u, d]) for u in range(3)
        ]

    @pl.when(step == 0)
    def _():
        for d in range(NX):
            grad_copy(d).start()

    @pl.when(here & (step == 0))
    def _():
        for d in range(NX):
            for copy in copies(d):
                copy.start()

    def update(d, master, moment_one, moment_two):
        gradient = grad[d].astype(F32)
        param = master[...].astype(F32)
        moment_new = beta_one * moment_one[...].astype(F32) + (1.0 - beta_one) * gradient
        second_new = beta_two * moment_two[...].astype(F32) + (1.0 - beta_two) * gradient * gradient
        scaled_one = moment_new / (1.0 - beta_one**STEP)
        scaled_two = second_new / (1.0 - beta_two**STEP)
        updated = param - learn_rate * (
            scaled_one / (jnp.sqrt(scaled_two) + adam_eps) + decay_rate * param
        )
        out_master[...] = updated
        out_one[...] = moment_new.astype(BF)
        out_two[...] = second_new.astype(BF)
        out_weight[...] = updated.astype(BF)

    for d in range(NX):

        @pl.when(step == d)
        def _():
            grad_copy(d).wait()

        @pl.when(here & (step == d))
        def _():
            for copy in copies(d):
                copy.wait()
            update(d, held.at[0, d], held.at[1, d], held.at[2, d])

    @pl.when(jnp.logical_not(here))
    def _():
        update(step, own_master, own_one, own_two)


def adam(plan, grads, own, came):
    rows, width = own[0].shape
    part = rows // NX
    spec = pl.BlockSpec((part, width), lambda i, plan: ((plan[MY_X] + i) % NX, 0))
    return pl.pallas_call(
        adam_kernel,
        out_shape=[jax.ShapeDtypeStruct((rows, width), d) for d in (F32, BF, BF, BF)],
        grid_spec=prefetch(
            (NX,),
            [spec] * 3 + [ANY] * (4 * NX),
            [spec] * 4,
            [
                pltpu.VMEM((NX, part, width), BF),
                pltpu.VMEM((3, NX, part, width), BF),
                pltpu.SemaphoreType.DMA((NX,)),
                pltpu.SemaphoreType.DMA((3, NX)),
            ],
        ),
        compiler_params=params(40),
    )(plan, *own, *grads, *(a for unit in came for a in unit))


def local(tokens_in, grad_out, token_counts, new_owner, master, moment_one, moment_two):
    place = jnp.stack([lax.axis_index("x"), lax.axis_index("z")]).astype(jnp.int32)
    own = (master[0], moment_one[0], moment_two[0])
    packed = pack(place, own)
    partial = partial_gradient(token_counts[0], tokens_in[0], grad_out[0], packed[0][:1])
    summed = lax.psum_scatter(partial, ("y", "core"), scatter_dimension=0, tiled=True)
    plan = make_plan(place, new_owner)
    came = relocate(plan, packed)
    (gradient,) = relocate(plan, pack(place, [summed]))
    outs = adam(plan, gradient, own, came)
    return tuple(o[None] for o in outs)


def solution(mesh):
    n_dp = mesh.devices.shape[0]
    fine = Mesh(mesh.devices.reshape(n_dp // 2, 2, NX, NZ), ("y", "core", "x", "z"))
    dp, expert = ("y", "core"), ("x", "z")
    whole = P(expert, dp, None)
    return jax.shard_map(
        local,
        mesh=fine,
        in_specs=(whole, whole, P(expert, dp), P(), whole, whole, whole),
        out_specs=(whole, whole, whole, whole),
        check_vma=False,
    )
```

```python
import functools

import jax
import jax.numpy as jnp
from jax import lax
from jax.experimental import pallas as pl
from jax.experimental.pallas import tpu as pltpu
from jax.sharding import Mesh, PartitionSpec as P

STEP = 10
NX = 4
NZ = 8
N = NX * NZ
UP = NZ // 2
DOWN = NZ - 1 - UP

beta_one = 0.9
beta_two = 0.95
learn_rate = 0.001
decay_rate = 0.1
adam_eps = 1e-08

BF = jnp.bfloat16
F32 = jnp.float32
ANY = pl.BlockSpec(memory_space=pl.ANY)
SMEM = pl.BlockSpec(memory_space=pltpu.SMEM)
VMEM = pl.BlockSpec(memory_space=pltpu.VMEM)


def hbm(arrays):
    return [pltpu.with_memory_space_constraint(a, pltpu.HBM) for a in arrays]


def vmem(arrays):
    return [pltpu.with_memory_space_constraint(a, pltpu.VMEM) for a in arrays]


def after_specs(after):
    return [SMEM if a.ndim == 1 else VMEM for a in after]


def after_args(after):
    return [a if a.ndim == 1 else vmem([a])[0] for a in after]


def params(mib):
    return pltpu.CompilerParams(vmem_limit_bytes=mib * 2**20)


def prefetch(grid, in_specs, out_specs, scratch=()):
    return pltpu.PrefetchScalarGridSpec(
        num_scalar_prefetch=1,
        grid=grid,
        in_specs=in_specs,
        out_specs=out_specs,
        scratch_shapes=scratch,
    )


def partial_kernel(n, count, tokens, grads, out, done, held, cotangents, masked, made, in_sems, out_sems):
    width = held.shape[2]

    def load(i):
        return pltpu.make_async_copy(tokens.at[:, pl.ds(i * width, width)], held.at[i], in_sems.at[i])

    def store(i):
        return pltpu.make_async_copy(made.at[i], out.at[pl.ds(i * width, width)], out_sems.at[i])

    load_grads = pltpu.make_async_copy(grads, cotangents, in_sems.at[n])
    load_grads.start()
    for i in range(n):
        load(i).start()
    load_grads.wait()
    live = lax.broadcasted_iota(jnp.int32, masked.shape, 0) < count[0]
    masked[...] = jnp.where(live, cotangents[...].astype(F32), 0.0).astype(BF)
    for i in range(n):
        load(i).wait()
        made[i] = jnp.dot(held[i].T, masked[...], preferred_element_type=F32).astype(BF)
        store(i).start()
    for i in range(n):
        store(i).wait()
    done[0] = 0


def partial_gradient(count, tokens, grads):
    cap, feats = tokens.shape
    ffw = grads.shape[1]
    n = 7
    return pl.pallas_call(
        functools.partial(partial_kernel, n),
        out_shape=[pltpu.HBM((feats, ffw), BF), jax.ShapeDtypeStruct((1,), jnp.int32)],
        grid_spec=prefetch(
            (1,),
            [ANY, ANY],
            [ANY, SMEM],
            [
                pltpu.VMEM((n, cap, feats // n), BF),
                pltpu.VMEM((cap, ffw), BF),
                pltpu.VMEM((cap, ffw), BF),
                pltpu.VMEM((n, feats // n, ffw), BF),
                pltpu.SemaphoreType.DMA((n + 1,)),
                pltpu.SemaphoreType.DMA((n,)),
            ],
        ),
        compiler_params=params(40),
    )(count, *hbm((tokens, grads)))


MY_X, MOVED, LEAVER, GO_UP, GO_DOWN, PICK = 0, 1, 2, 3, 4, 5


def plan_kernel(place, new_owner, out):
    my_x, my_z = place[0], place[1]
    me = my_x * NZ + my_z
    leaver, moved, up, down = jnp.int32(0), jnp.int32(0), jnp.int32(0), jnp.int32(0)
    for e in range(N):
        to = new_owner[e]
        x, z = e // NZ, e % NZ
        away = (to + NZ - z) % NZ
        mine = (my_z == z) & (away != 0)
        dist = (x + NX - my_x) % NX
        leaver += jnp.where(mine, dist, 0)
        up += jnp.where(mine & (away <= UP), 1, 0)
        down += jnp.where(mine & (away > UP), 1, 0)
        moved += jnp.where((to == me) & (to != e), 1, 0)

        @pl.when(to % NZ == my_z)
        def _():
            along = jnp.where(away <= UP, NX - 1 + away, NX + UP + NZ - 1 - away)
            out[PICK + (to // NZ + NX - my_x) % NX] = jnp.where(away == 0, dist, along)

    out[MY_X] = my_x
    out[MOVED] = moved
    out[LEAVER] = leaver
    out[GO_UP] = up
    out[GO_DOWN] = down


def make_plan(place, new_owner):
    return pl.pallas_call(
        plan_kernel,
        out_shape=jax.ShapeDtypeStruct((PICK + NX,), jnp.int32),
        in_specs=[SMEM] * 2,
        out_specs=SMEM,
    )(place, new_owner)


def pack_kernel(n, place, *refs):
    own, outs, (held, sems) = refs[:n], refs[-2 - n * NX : -2], refs[-2:]
    part = outs[0].shape[0]

    def load(u, d):
        start = pl.multiple_of((place[0] + d) % NX * part, part)
        return pltpu.make_async_copy(
            own[u].at[pl.ds(start, part)],
            held.at[d] if own[u].dtype == F32 else outs[u * NX + d],
            sems.at[u, d],
        )

    for u in range(n):
        for d in range(NX):
            load(u, d).start()
    for u in range(n):
        for d in range(NX):
            load(u, d).wait()
            if own[u].dtype == F32:
                outs[u * NX + d][...] = held[d].astype(BF)


def pack(place, own, after=()):
    rows, width = own[0].shape
    part, n = rows // NX, len(own)
    made = pl.pallas_call(
        functools.partial(pack_kernel, n),
        out_shape=[pltpu.VMEM((part, width), BF)] * (NX * n),
        in_specs=[SMEM] + [ANY] * n + after_specs(after),
        out_specs=[VMEM] * (NX * n),
        scratch_shapes=[pltpu.VMEM((NX, part, width), F32), pltpu.SemaphoreType.DMA((n, NX))],
        compiler_params=params(16),
    )(place, *hbm(own), *after_args(after))
    return [made[u * NX : (u + 1) * NX] for u in range(n)]


def pick_kernel(n, which, n_out, plan, *refs):
    cases, outs, done = refs[:n], refs[-1 - n_out : -1], refs[-1]
    for out, chosen in zip(outs, which(plan)):
        for c in range(n):

            @pl.when(chosen == c)
            def _():
                out[...] = cases[c][...]

    done[0] = 0


def pick(plan, which, n_out, cases, after=()):
    shape = cases[0].shape
    return pl.pallas_call(
        functools.partial(pick_kernel, len(cases), which, n_out),
        out_shape=[pltpu.VMEM(shape, BF)] * n_out + [jax.ShapeDtypeStruct((1,), jnp.int32)],
        in_specs=[SMEM] + [VMEM] * len(cases) + after_specs(after),
        out_specs=[VMEM] * n_out + [SMEM],
        compiler_params=params(16),
    )(plan, *vmem(cases), *after_args(after))


def ring(a, axis, size, by):
    return lax.ppermute(a, axis, [(i, (i + by) % size) for i in range(size)])


def swap_x(pieces):
    came = list(pieces)
    for d in (1, 3, 2):
        came[(-d) % NX] = ring(pieces[d], "x", NX, d)
    return came


def along_z(plan, spreads):
    n = len(spreads)
    first, done = pick(plan, lambda plan: [plan[LEAVER]], 1, spreads[0])
    ups, downs = [ring(first, "z", NZ, 1)], [ring(first, "z", NZ, -1)]

    def own_or_passed(plan):
        return [
            jnp.where(plan[GO_UP] != 0, plan[LEAVER], NX),
            jnp.where(plan[GO_DOWN] != 0, plan[LEAVER], NX + 1),
        ]

    for t in range(1, n):
        up, down, done = pick(plan, own_or_passed, 2, [*spreads[t], ups[-1], downs[-1]])
        ups.append(ring(up, "z", NZ, 1))
        downs.append(ring(down, "z", NZ, -1))
    while len(ups) < n + UP - 1:
        ups.append(ring(ups[-1], "z", NZ, 1))
    while len(downs) < n + DOWN - 1:
        downs.append(ring(downs[-1], "z", NZ, -1))
    return [ups[j : j + UP] + downs[j : j + DOWN] for j in range(n)], done


def deliver(plan, spread, came, after=()):
    def delivered(plan):
        return [plan[PICK + d] for d in range(NX)]

    return swap_x(pick(plan, delivered, NX, [*spread, *came], after)[:NX])


def adam_kernel(plan, own_master, own_one, own_two, *refs):
    grads, masters, ones, twos = (refs[k * NX : (k + 1) * NX] for k in range(4))
    out_master, out_one, out_two, out_weight = refs[4 * NX :]
    step = pl.program_id(0)
    here = plan[MOVED] != 0

    def update(d, master, moment_one, moment_two):
        gradient = grads[d][...].astype(F32)
        param = master[...].astype(F32)
        moment_new = beta_one * moment_one[...].astype(F32) + (1.0 - beta_one) * gradient
        second_new = beta_two * moment_two[...].astype(F32) + (1.0 - beta_two) * gradient * gradient
        scaled_one = moment_new / (1.0 - beta_one**STEP)
        scaled_two = second_new / (1.0 - beta_two**STEP)
        updated = param - learn_rate * (
            scaled_one / (jnp.sqrt(scaled_two) + adam_eps) + decay_rate * param
        )
        out_master[...] = updated
        out_one[...] = moment_new.astype(BF)
        out_two[...] = second_new.astype(BF)
        out_weight[...] = updated.astype(BF)

    for d in range(NX):

        @pl.when(here & (step == d))
        def _():
            update(d, masters[d], ones[d], twos[d])

        @pl.when(jnp.logical_not(here) & (step == d))
        def _():
            update(d, own_master, own_one, own_two)


def adam(plan, grads, own, came):
    rows, width = own[0].shape
    part = rows // NX
    spec = pl.BlockSpec((part, width), lambda i, plan: ((plan[MY_X] + i) % NX, 0))
    moved = [a for unit in (grads, *came) for a in unit]
    return pl.pallas_call(
        adam_kernel,
        out_shape=[jax.ShapeDtypeStruct((rows, width), d) for d in (F32, BF, BF, BF)],
        grid_spec=prefetch((NX,), [spec] * 3 + [VMEM] * len(moved), [spec] * 4),
        compiler_params=params(40),
    )(plan, *hbm(own), *vmem(moved))


def local(tokens_in, grad_out, token_counts, new_owner, master, moment_one, moment_two):
    place = jnp.stack([lax.axis_index("x"), lax.axis_index("z")]).astype(jnp.int32)
    own = (master[0], moment_one[0], moment_two[0])
    partial, made = partial_gradient(token_counts[0], tokens_in[0], grad_out[0])
    summed = lax.psum_scatter(partial, ("y", "core"), scatter_dimension=0, tiled=True)
    plan = make_plan(place, new_owner)

    spreads = [swap_x(pieces) for pieces in pack(place, own, [made])]
    rows, _ = along_z(plan, spreads)
    grad_spread = swap_x(pack(place, [summed], [rows[2][0], rows[2][UP]])[0])
    (grad_rows,), gone = along_z(plan, [grad_spread])
    came = [deliver(plan, *pair, [gone]) for pair in zip(spreads, rows)]
    gradient = deliver(plan, grad_spread, grad_rows, [*came[0][1:], *came[1][1:]])
    outs = adam(plan, gradient, own, came)
    return tuple(o[None] for o in outs)


def solution(mesh):
    n_dp = mesh.devices.shape[0]
    fine = Mesh(mesh.devices.reshape(n_dp // 2, 2, NX, NZ), ("y", "core", "x", "z"))
    dp, expert = ("y", "core"), ("x", "z")
    whole = P(expert, dp, None)
    return jax.shard_map(
        local,
        mesh=fine,
        in_specs=(whole, whole, P(expert, dp), P(), whole, whole, whole),
        out_specs=(whole, whole, whole, whole),
        check_vma=False,
    )
```

```python
import functools

import jax
import jax.numpy as jnp
from jax import lax
from jax.experimental import pallas as pl
from jax.experimental.pallas import tpu as pltpu
from jax.sharding import Mesh, PartitionSpec as P

STEP = 10
NX = 4
NZ = 8
N = NX * NZ
UP = NZ // 2
DOWN = NZ - 1 - UP

beta_one = 0.9
beta_two = 0.95
learn_rate = 0.001
decay_rate = 0.1
adam_eps = 1e-08

BF = jnp.bfloat16
F32 = jnp.float32
ANY = pl.BlockSpec(memory_space=pl.ANY)
SMEM = pl.BlockSpec(memory_space=pltpu.SMEM)
VMEM = pl.BlockSpec(memory_space=pltpu.VMEM)


def hbm(arrays):
    return [pltpu.with_memory_space_constraint(a, pltpu.HBM) for a in arrays]


def vmem(arrays):
    return [pltpu.with_memory_space_constraint(a, pltpu.VMEM) for a in arrays]


def after_specs(after):
    return [SMEM if a.ndim == 1 else VMEM for a in after]


def after_args(after):
    return [a if a.ndim == 1 else vmem([a])[0] for a in after]


def params(mib):
    return pltpu.CompilerParams(vmem_limit_bytes=mib * 2**20)


def prefetch(grid, in_specs, out_specs, scratch=()):
    return pltpu.PrefetchScalarGridSpec(
        num_scalar_prefetch=1,
        grid=grid,
        in_specs=in_specs,
        out_specs=out_specs,
        scratch_shapes=scratch,
    )


def partial_kernel(n, count, tokens, grads, out, done, held, cotangents, masked, made, in_sems, out_sems):
    width = held.shape[2]

    def load(i):
        return pltpu.make_async_copy(tokens.at[:, pl.ds(i * width, width)], held.at[i], in_sems.at[i])

    def store(i):
        return pltpu.make_async_copy(made.at[i], out.at[pl.ds(i * width, width)], out_sems.at[i])

    load_grads = pltpu.make_async_copy(grads, cotangents, in_sems.at[n])
    load_grads.start()
    for i in range(n):
        load(i).start()
    load_grads.wait()
    live = lax.broadcasted_iota(jnp.int32, masked.shape, 0) < count[0]
    masked[...] = jnp.where(live, cotangents[...].astype(F32), 0.0).astype(BF)
    for i in range(n):
        load(i).wait()
        made[i] = jnp.dot(held[i].T, masked[...], preferred_element_type=F32).astype(BF)
        store(i).start()
    for i in range(n):
        store(i).wait()
    done[0] = 0


def partial_gradient(count, tokens, grads):
    cap, feats = tokens.shape
    ffw = grads.shape[1]
    n = 7
    return pl.pallas_call(
        functools.partial(partial_kernel, n),
        out_shape=[pltpu.HBM((feats, ffw), BF), jax.ShapeDtypeStruct((1,), jnp.int32)],
        grid_spec=prefetch(
            (1,),
            [ANY, ANY],
            [ANY, SMEM],
            [
                pltpu.VMEM((n, cap, feats // n), BF),
                pltpu.VMEM((cap, ffw), BF),
                pltpu.VMEM((cap, ffw), BF),
                pltpu.VMEM((n, feats // n, ffw), BF),
                pltpu.SemaphoreType.DMA((n + 1,)),
                pltpu.SemaphoreType.DMA((n,)),
            ],
        ),
        compiler_params=params(40),
    )(count, *hbm((tokens, grads)))


MY_X, MOVED, LEAVER, GO_UP, GO_DOWN, PICK = 0, 1, 2, 3, 4, 5
FAR_UP, FAR_DOWN, PICK_FAR = PICK + NX, PICK + NX + 1, PICK + NX + 2


def plan_kernel(place, new_owner, out):
    my_x, my_z = place[0], place[1]
    me = my_x * NZ + my_z
    leaver, moved, up, down = jnp.int32(0), jnp.int32(0), jnp.int32(0), jnp.int32(0)
    far_up, far_down = jnp.int32(0), jnp.int32(0)
    for e in range(N):
        to = new_owner[e]
        x, z = e // NZ, e % NZ
        away = (to + NZ - z) % NZ
        mine = (my_z == z) & (away != 0)
        dist = (x + NX - my_x) % NX
        leaver += jnp.where(mine, dist, 0)
        up += jnp.where(mine & (away <= UP), 1, 0)
        down += jnp.where(mine & (away > UP), 1, 0)
        moved += jnp.where((to == me) & (to != e), 1, 0)

        above, below = (z + 1) % NZ == my_z, (z + NZ - 1) % NZ == my_z
        far_up += jnp.where((my_z == z) & (away == 3), dist, 0)
        far_up += jnp.where(above & (away == 4), NX, 0) + jnp.where(below & (away == 2), NX + 1, 0)
        far_down += jnp.where((my_z == z) & (away == NZ - 3), dist, 0)
        far_down += jnp.where(above & (away == NZ - 2), NX, 0)

        @pl.when(to % NZ == my_z)
        def _():
            near = jnp.where(away == 1, NX, NX + 1)
            far = jnp.where(away <= UP, NX + 2, NX + 3)
            hop = jnp.where((away == 1) | (away == NZ - 1), near, far)
            out[PICK_FAR + (to // NZ + NX - my_x) % NX] = jnp.where(away == 0, dist, hop)
            along = jnp.where(away <= UP, NX - 1 + away, NX + UP + NZ - 1 - away)
            out[PICK + (to // NZ + NX - my_x) % NX] = jnp.where(away == 0, dist, along)

    out[MY_X] = my_x
    out[MOVED] = moved
    out[LEAVER] = leaver
    out[GO_UP] = up
    out[GO_DOWN] = down
    out[FAR_UP] = far_up
    out[FAR_DOWN] = far_down


def make_plan(place, new_owner):
    return pl.pallas_call(
        plan_kernel,
        out_shape=jax.ShapeDtypeStruct((PICK_FAR + NX,), jnp.int32),
        in_specs=[SMEM] * 2,
        out_specs=SMEM,
    )(place, new_owner)


def pack_kernel(n, place, *refs):
    own, outs, (held, sems) = refs[:n], refs[-2 - n * NX : -2], refs[-2:]
    part = outs[0].shape[0]

    def load(u, d):
        start = pl.multiple_of((place[0] + d) % NX * part, part)
        return pltpu.make_async_copy(
            own[u].at[pl.ds(start, part)],
            held.at[d] if own[u].dtype == F32 else outs[u * NX + d],
            sems.at[u, d],
        )

    for u in range(n):
        for d in range(NX):
            load(u, d).start()
    for u in range(n):
        for d in range(NX):
            load(u, d).wait()
            if own[u].dtype == F32:
                outs[u * NX + d][...] = held[d].astype(BF)


def pack(place, own, after=()):
    rows, width = own[0].shape
    part, n = rows // NX, len(own)
    made = pl.pallas_call(
        functools.partial(pack_kernel, n),
        out_shape=[pltpu.VMEM((part, width), BF)] * (NX * n),
        in_specs=[SMEM] + [ANY] * n + after_specs(after),
        out_specs=[VMEM] * (NX * n),
        scratch_shapes=[pltpu.VMEM((NX, part, width), F32), pltpu.SemaphoreType.DMA((n, NX))],
        compiler_params=params(16),
    )(place, *hbm(own), *after_args(after))
    return [made[u * NX : (u + 1) * NX] for u in range(n)]


def pick_kernel(n, which, n_out, plan, *refs):
    cases, outs, done = refs[:n], refs[-1 - n_out : -1], refs[-1]
    for out, chosen in zip(outs, which(plan)):
        for c in range(n):

            @pl.when(chosen == c)
            def _():
                out[...] = cases[c][...]

    done[0] = 0


def pick(plan, which, n_out, cases, after=()):
    shape = cases[0].shape
    return pl.pallas_call(
        functools.partial(pick_kernel, len(cases), which, n_out),
        out_shape=[pltpu.VMEM(shape, BF)] * n_out + [jax.ShapeDtypeStruct((1,), jnp.int32)],
        in_specs=[SMEM] + [VMEM] * len(cases) + after_specs(after),
        out_specs=[VMEM] * n_out + [SMEM],
        compiler_params=params(16),
    )(plan, *vmem(cases), *after_args(after))


def ring(a, axis, size, by):
    return lax.ppermute(a, axis, [(i, (i + by) % size) for i in range(size)])


def swap_x(pieces):
    came = list(pieces)
    for d in (1, 3, 2):
        came[(-d) % NX] = ring(pieces[d], "x", NX, d)
    return came


def along_z(plan, spreads):
    n = len(spreads)
    first, done = pick(plan, lambda plan: [plan[LEAVER]], 1, spreads[0])
    ups, downs = [ring(first, "z", NZ, 1)], [ring(first, "z", NZ, -1)]

    def own_or_passed(plan):
        return [
            jnp.where(plan[GO_UP] != 0, plan[LEAVER], NX),
            jnp.where(plan[GO_DOWN] != 0, plan[LEAVER], NX + 1),
        ]

    for t in range(1, n):
        up, down, done = pick(plan, own_or_passed, 2, [*spreads[t], ups[-1], downs[-1]])
        ups.append(ring(up, "z", NZ, 1))
        downs.append(ring(down, "z", NZ, -1))
    while len(ups) < n + UP - 1:
        ups.append(ring(ups[-1], "z", NZ, 1))
    while len(downs) < n + DOWN - 1:
        downs.append(ring(downs[-1], "z", NZ, -1))
    return [ups[j : j + UP] + downs[j : j + DOWN] for j in range(n)], done


def hop_near(plan, spread, after):
    first, done = pick(plan, lambda plan: [plan[LEAVER]], 1, spread, after)
    return [ring(first, "z", NZ, 1), ring(first, "z", NZ, -1)], done


def hop_far(plan, spread, near, after):
    up, down, done = pick(
        plan, lambda plan: [plan[FAR_UP], plan[FAR_DOWN]], 2, [*spread, *near], after
    )
    return [ring(up, "z", NZ, 3), ring(down, "z", NZ, -3)], done


def deliver(plan, at, spread, came, after=()):
    def delivered(plan):
        return [plan[at + d] for d in range(NX)]

    *pieces, done = pick(plan, delivered, NX, [*spread, *came], after)
    return swap_x(pieces), done


def adam_kernel(plan, own_master, own_one, own_two, *refs):
    grads, masters, ones, twos = (refs[k * NX : (k + 1) * NX] for k in range(4))
    out_master, out_one, out_two, out_weight = refs[4 * NX :]
    step = pl.program_id(0)
    here = plan[MOVED] != 0

    def update(d, master, moment_one, moment_two):
        gradient = grads[d][...].astype(F32)
        param = master[...].astype(F32)
        moment_new = beta_one * moment_one[...].astype(F32) + (1.0 - beta_one) * gradient
        second_new = beta_two * moment_two[...].astype(F32) + (1.0 - beta_two) * gradient * gradient
        scaled_one = moment_new / (1.0 - beta_one**STEP)
        scaled_two = second_new / (1.0 - beta_two**STEP)
        updated = param - learn_rate * (
            scaled_one / (jnp.sqrt(scaled_two) + adam_eps) + decay_rate * param
        )
        out_master[...] = updated
        out_one[...] = moment_new.astype(BF)
        out_two[...] = second_new.astype(BF)
        out_weight[...] = updated.astype(BF)

    for d in range(NX):

        @pl.when(here & (step == d))
        def _():
            update(d, masters[d], ones[d], twos[d])

        @pl.when(jnp.logical_not(here) & (step == d))
        def _():
            update(d, own_master, own_one, own_two)


def adam(plan, grads, own, came):
    rows, width = own[0].shape
    part = rows // NX
    spec = pl.BlockSpec((part, width), lambda i, plan: ((plan[MY_X] + i) % NX, 0))
    moved = [a for unit in (grads, *came) for a in unit]
    return pl.pallas_call(
        adam_kernel,
        out_shape=[jax.ShapeDtypeStruct((rows, width), d) for d in (F32, BF, BF, BF)],
        grid_spec=prefetch((NX,), [spec] * 3 + [VMEM] * len(moved), [spec] * 4),
        compiler_params=params(40),
    )(plan, *hbm(own), *vmem(moved))


def local(tokens_in, grad_out, token_counts, new_owner, master, moment_one, moment_two):
    place = jnp.stack([lax.axis_index("x"), lax.axis_index("z")]).astype(jnp.int32)
    own = (master[0], moment_one[0], moment_two[0])
    partial, made = partial_gradient(token_counts[0], tokens_in[0], grad_out[0])
    summed = lax.psum_scatter(partial, ("y", "core"), scatter_dimension=0, tiled=True)
    plan = make_plan(place, new_owner)

    spreads = [swap_x(pieces) for pieces in pack(place, own, [made])]
    rows, _ = along_z(plan, spreads)
    grad_spread = swap_x(pack(place, [summed], [rows[2][0], rows[2][UP]])[0])
    came_0, done = deliver(plan, PICK, spreads[0], rows[0])
    near, done = hop_near(plan, grad_spread, [done])
    came_1, done = deliver(plan, PICK, spreads[1], rows[1], [done])
    far, done = hop_far(plan, grad_spread, near, [done])
    came_2, _ = deliver(plan, PICK, spreads[2], rows[2], [done])
    ahead = [*came_0[1:], *came_1[1:]]
    gradient, _ = deliver(plan, PICK_FAR, grad_spread, near + far, ahead)
    outs = adam(plan, gradient, own, (came_0, came_1, came_2))
    return tuple(o[None] for o in outs)


def solution(mesh):
    n_dp = mesh.devices.shape[0]
    fine = Mesh(mesh.devices.reshape(n_dp // 2, 2, NX, NZ), ("y", "core", "x", "z"))
    dp, expert = ("y", "core"), ("x", "z")
    whole = P(expert, dp, None)
    return jax.shard_map(
        local,
        mesh=fine,
        in_specs=(whole, whole, P(expert, dp), P(), whole, whole, whole),
        out_specs=(whole, whole, whole, whole),
        check_vma=False,
    )
```

```python
import functools

import jax
import jax.numpy as jnp
from jax import lax
from jax.experimental import pallas as pl
from jax.experimental.pallas import tpu as pltpu
from jax.sharding import Mesh, PartitionSpec as P

STEP = 10
NX = 4
NZ = 8
N = NX * NZ
UP = NZ // 2
DOWN = NZ - 1 - UP

beta_one = 0.9
beta_two = 0.95
learn_rate = 0.001
decay_rate = 0.1
adam_eps = 1e-08

BF = jnp.bfloat16
F32 = jnp.float32
ANY = pl.BlockSpec(memory_space=pl.ANY)
SMEM = pl.BlockSpec(memory_space=pltpu.SMEM)
VMEM = pl.BlockSpec(memory_space=pltpu.VMEM)


def hbm(arrays):
    return [pltpu.with_memory_space_constraint(a, pltpu.HBM) for a in arrays]


def vmem(arrays):
    return [pltpu.with_memory_space_constraint(a, pltpu.VMEM) for a in arrays]


def after_specs(after):
    return [SMEM if a.ndim == 1 else VMEM for a in after]


def after_args(after):
    return [a if a.ndim == 1 else vmem([a])[0] for a in after]


def params(mib):
    return pltpu.CompilerParams(vmem_limit_bytes=mib * 2**20)


def prefetch(grid, in_specs, out_specs, scratch=()):
    return pltpu.PrefetchScalarGridSpec(
        num_scalar_prefetch=1,
        grid=grid,
        in_specs=in_specs,
        out_specs=out_specs,
        scratch_shapes=scratch,
    )


def partial_kernel(n, count, tokens, grads, out, done, held, cotangents, masked, made, in_sems, out_sems):
    width = held.shape[2]

    def load(i):
        return pltpu.make_async_copy(tokens.at[:, pl.ds(i * width, width)], held.at[i], in_sems.at[i])

    def store(i):
        return pltpu.make_async_copy(made.at[i], out.at[pl.ds(i * width, width)], out_sems.at[i])

    load_grads = pltpu.make_async_copy(grads, cotangents, in_sems.at[n])
    load_grads.start()
    for i in range(n):
        load(i).start()
    load_grads.wait()
    live = lax.broadcasted_iota(jnp.int32, masked.shape, 0) < count[0]
    masked[...] = jnp.where(live, cotangents[...].astype(F32), 0.0).astype(BF)
    for i in range(n):
        load(i).wait()
        made[i] = jnp.dot(held[i].T, masked[...], preferred_element_type=F32).astype(BF)
        store(i).start()
    for i in range(n):
        store(i).wait()
    done[0] = 0


def partial_gradient(count, tokens, grads):
    cap, feats = tokens.shape
    ffw = grads.shape[1]
    n = 7
    return pl.pallas_call(
        functools.partial(partial_kernel, n),
        out_shape=[pltpu.HBM((feats, ffw), BF), jax.ShapeDtypeStruct((1,), jnp.int32)],
        grid_spec=prefetch(
            (1,),
            [ANY, ANY],
            [ANY, SMEM],
            [
                pltpu.VMEM((n, cap, feats // n), BF),
                pltpu.VMEM((cap, ffw), BF),
                pltpu.VMEM((cap, ffw), BF),
                pltpu.VMEM((n, feats // n, ffw), BF),
                pltpu.SemaphoreType.DMA((n + 1,)),
                pltpu.SemaphoreType.DMA((n,)),
            ],
        ),
        compiler_params=params(40),
    )(count, *hbm((tokens, grads)))


MY_X, MOVED, LEAVER, GO_UP, GO_DOWN, PICK = 0, 1, 2, 3, 4, 5
FAR_UP, FAR_DOWN, PICK_FAR = PICK + NX, PICK + NX + 1, PICK + NX + 2


def plan_kernel(place, new_owner, out):
    my_x, my_z = place[0], place[1]
    me = my_x * NZ + my_z
    leaver, moved, up, down = jnp.int32(0), jnp.int32(0), jnp.int32(0), jnp.int32(0)
    far_up, far_down = jnp.int32(0), jnp.int32(0)
    for e in range(N):
        to = new_owner[e]
        x, z = e // NZ, e % NZ
        away = (to + NZ - z) % NZ
        mine = (my_z == z) & (away != 0)
        dist = (x + NX - my_x) % NX
        leaver += jnp.where(mine, dist, 0)
        up += jnp.where(mine & (away <= UP), 1, 0)
        down += jnp.where(mine & (away > UP), 1, 0)
        moved += jnp.where((to == me) & (to != e), 1, 0)

        above, below = (z + 1) % NZ == my_z, (z + NZ - 1) % NZ == my_z
        far_up += jnp.where((my_z == z) & (away == 3), dist, 0)
        far_up += jnp.where(above & (away == 4), NX, 0) + jnp.where(below & (away == 2), NX + 1, 0)
        far_down += jnp.where((my_z == z) & (away == NZ - 3), dist, 0)
        far_down += jnp.where(above & (away == NZ - 2), NX, 0)

        @pl.when(to % NZ == my_z)
        def _():
            near = jnp.where(away == 1, NX, NX + 1)
            far = jnp.where(away <= UP, NX + 2, NX + 3)
            hop = jnp.where((away == 1) | (away == NZ - 1), near, far)
            out[PICK_FAR + (to // NZ + NX - my_x) % NX] = jnp.where(away == 0, dist, hop)
            along = jnp.where(away <= UP, NX - 1 + away, NX + UP + NZ - 1 - away)
            out[PICK + (to // NZ + NX - my_x) % NX] = jnp.where(away == 0, dist, along)

    out[MY_X] = my_x
    out[MOVED] = moved
    out[LEAVER] = leaver
    out[GO_UP] = up
    out[GO_DOWN] = down
    out[FAR_UP] = far_up
    out[FAR_DOWN] = far_down


def make_plan(place, new_owner):
    return pl.pallas_call(
        plan_kernel,
        out_shape=jax.ShapeDtypeStruct((PICK_FAR + NX,), jnp.int32),
        in_specs=[SMEM] * 2,
        out_specs=SMEM,
    )(place, new_owner)


def pack_kernel(n, place, *refs):
    own, outs, (held, sems) = refs[:n], refs[-2 - n * NX : -2], refs[-2:]
    part = outs[0].shape[0]

    def load(u, d):
        start = pl.multiple_of((place[0] + d) % NX * part, part)
        return pltpu.make_async_copy(
            own[u].at[pl.ds(start, part)],
            held.at[d] if own[u].dtype == F32 else outs[u * NX + d],
            sems.at[u, d],
        )

    for u in range(n):
        for d in range(NX):
            load(u, d).start()
    for u in range(n):
        for d in range(NX):
            load(u, d).wait()
            if own[u].dtype == F32:
                outs[u * NX + d][...] = held[d].astype(BF)


def pack(place, own, after=()):
    rows, width = own[0].shape
    part, n = rows // NX, len(own)
    made = pl.pallas_call(
        functools.partial(pack_kernel, n),
        out_shape=[pltpu.VMEM((part, width), BF)] * (NX * n),
        in_specs=[SMEM] + [ANY] * n + after_specs(after),
        out_specs=[VMEM] * (NX * n),
        scratch_shapes=[pltpu.VMEM((NX, part, width), F32), pltpu.SemaphoreType.DMA((n, NX))],
        compiler_params=params(16),
    )(place, *hbm(own), *after_args(after))
    return [made[u * NX : (u + 1) * NX] for u in range(n)]


def pick_kernel(n, which, n_out, plan, *refs):
    cases, outs, done = refs[:n], refs[-1 - n_out : -1], refs[-1]
    for out, chosen in zip(outs, which(plan)):
        for c in range(n):

            @pl.when(chosen == c)
            def _():
                out[...] = cases[c][...]

    done[0] = 0


def pick(plan, which, n_out, cases, after=()):
    shape = cases[0].shape
    return pl.pallas_call(
        functools.partial(pick_kernel, len(cases), which, n_out),
        out_shape=[pltpu.VMEM(shape, BF)] * n_out + [jax.ShapeDtypeStruct((1,), jnp.int32)],
        in_specs=[SMEM] + [VMEM] * len(cases) + after_specs(after),
        out_specs=[VMEM] * n_out + [SMEM],
        compiler_params=params(16),
    )(plan, *vmem(cases), *after_args(after))


def ring(a, axis, size, by):
    return lax.ppermute(a, axis, [(i, (i + by) % size) for i in range(size)])


def swap_x(pieces):
    came = list(pieces)
    for d in (1, 3, 2):
        came[(-d) % NX] = ring(pieces[d], "x", NX, d)
    return came


def along_z(plan, spreads):
    n = len(spreads)
    first, done = pick(plan, lambda plan: [plan[LEAVER]], 1, spreads[0])
    ups, downs = [ring(first, "z", NZ, 1)], [ring(first, "z", NZ, -1)]

    def own_or_passed(plan):
        return [
            jnp.where(plan[GO_UP] != 0, plan[LEAVER], NX),
            jnp.where(plan[GO_DOWN] != 0, plan[LEAVER], NX + 1),
        ]

    for t in range(1, n):
        up, down, done = pick(plan, own_or_passed, 2, [*spreads[t], ups[-1], downs[-1]])
        ups.append(ring(up, "z", NZ, 1))
        downs.append(ring(down, "z", NZ, -1))
    while len(ups) < n + UP - 1:
        ups.append(ring(ups[-1], "z", NZ, 1))
    while len(downs) < n + DOWN - 1:
        downs.append(ring(downs[-1], "z", NZ, -1))
    return [ups[j : j + UP] + downs[j : j + DOWN] for j in range(n)], done


def hop_near(plan, spread, after):
    first, done = pick(plan, lambda plan: [plan[LEAVER]], 1, spread, after)
    return [ring(first, "z", NZ, 1), ring(first, "z", NZ, -1)], done


def hop_far(plan, spread, near, after):
    up, down, done = pick(
        plan, lambda plan: [plan[FAR_UP], plan[FAR_DOWN]], 2, [*spread, *near], after
    )
    return [ring(up, "z", NZ, 3), ring(down, "z", NZ, -3)], done


def deliver(plan, at, spread, came, after=()):
    def delivered(plan):
        return [plan[at + d] for d in range(NX)]

    *pieces, done = pick(plan, delivered, NX, [*spread, *came], after)
    return swap_x(pieces), done


def adam_kernel(n, plan, own_master, own_one, own_two, *refs):
    grads, masters, ones, twos = (refs[k * n : (k + 1) * n] for k in range(4))
    out_master, out_one, out_two, out_weight = refs[-4:]
    step = pl.program_id(0)
    here = plan[MOVED] != 0

    def update(d, master, moment_one, moment_two):
        gradient = grads[d][...].astype(F32)
        param = master[...].astype(F32)
        moment_new = beta_one * moment_one[...].astype(F32) + (1.0 - beta_one) * gradient
        second_new = beta_two * moment_two[...].astype(F32) + (1.0 - beta_two) * gradient * gradient
        scaled_one = moment_new / (1.0 - beta_one**STEP)
        scaled_two = second_new / (1.0 - beta_two**STEP)
        updated = param - learn_rate * (
            scaled_one / (jnp.sqrt(scaled_two) + adam_eps) + decay_rate * param
        )
        out_master[...] = updated
        out_one[...] = moment_new.astype(BF)
        out_two[...] = second_new.astype(BF)
        out_weight[...] = updated.astype(BF)

    for d in range(n):

        @pl.when(here & (step == d))
        def _():
            update(d, masters[d], ones[d], twos[d])

        @pl.when(jnp.logical_not(here) & (step == d))
        def _():
            update(d, own_master, own_one, own_two)


def adam(plan, first, n, grads, own, came, before=(), after=()):
    rows, width = own[0].shape
    part = rows // NX
    spec = pl.BlockSpec((part, width), lambda i, plan: ((plan[MY_X] + first + i) % NX, 0))
    moved = [a for unit in (grads, *came) for a in unit[first : first + n]]
    return pl.pallas_call(
        functools.partial(adam_kernel, n),
        out_shape=[jax.ShapeDtypeStruct((rows, width), d) for d in (F32, BF, BF, BF)],
        grid_spec=prefetch(
            (n,), [spec] * 3 + [VMEM] * len(moved) + [ANY] * len(before) + after_specs(after), [spec] * 4
        ),
        input_output_aliases={4 + len(moved) + k: k for k in range(len(before))},
        compiler_params=params(24),
    )(plan, *hbm(own), *vmem(moved), *before, *after_args(after))


def local(tokens_in, grad_out, token_counts, new_owner, master, moment_one, moment_two):
    place = jnp.stack([lax.axis_index("x"), lax.axis_index("z")]).astype(jnp.int32)
    own = (master[0], moment_one[0], moment_two[0])
    partial, made = partial_gradient(token_counts[0], tokens_in[0], grad_out[0])
    summed = lax.psum_scatter(partial, ("y", "core"), scatter_dimension=0, tiled=True)
    plan = make_plan(place, new_owner)

    packed = pack(place, own[1:2], [made]) + pack(place, [own[2], own[0]], [plan])
    spreads = [swap_x(pieces) for pieces in packed]
    rows, _ = along_z(plan, spreads)
    grad_spread = swap_x(pack(place, [summed], [rows[2][0], rows[2][UP]])[0])
    came_0, done = deliver(plan, PICK, spreads[0], rows[0])
    near, done = hop_near(plan, grad_spread, [done])
    came_1, done = deliver(plan, PICK, spreads[1], rows[1], [done])
    far, done = hop_far(plan, grad_spread, near, [done])
    came_2, _ = deliver(plan, PICK, spreads[2], rows[2], [done])
    ahead = [*came_0[1:], *came_1[1:]]
    gradient, _ = deliver(plan, PICK_FAR, grad_spread, near + far, ahead)
    came = (came_2, came_0, came_1)
    outs = adam(plan, 0, 2, gradient, own, came, after=came_2[2:])
    outs = adam(plan, 2, 2, gradient, own, came, outs)
    return tuple(o[None] for o in outs)


def solution(mesh):
    n_dp = mesh.devices.shape[0]
    fine = Mesh(mesh.devices.reshape(n_dp // 2, 2, NX, NZ), ("y", "core", "x", "z"))
    dp, expert = ("y", "core"), ("x", "z")
    whole = P(expert, dp, None)
    return jax.shard_map(
        local,
        mesh=fine,
        in_specs=(whole, whole, P(expert, dp), P(), whole, whole, whole),
        out_specs=(whole, whole, whole, whole),
        check_vma=False,
    )
```

```python
import functools

import jax
import jax.numpy as jnp
from jax import lax
from jax.experimental import pallas as pl
from jax.experimental.pallas import tpu as pltpu
from jax.sharding import Mesh, PartitionSpec as P

STEP = 10
NX = 4
NZ = 8
N = NX * NZ
UP = NZ // 2
DOWN = NZ - 1 - UP

beta_one = 0.9
beta_two = 0.95
learn_rate = 0.001
decay_rate = 0.1
adam_eps = 1e-08

BF = jnp.bfloat16
F32 = jnp.float32
ANY = pl.BlockSpec(memory_space=pl.ANY)
SMEM = pl.BlockSpec(memory_space=pltpu.SMEM)
VMEM = pl.BlockSpec(memory_space=pltpu.VMEM)


def hbm(arrays):
    return [pltpu.with_memory_space_constraint(a, pltpu.HBM) for a in arrays]


def vmem(arrays):
    return [pltpu.with_memory_space_constraint(a, pltpu.VMEM) for a in arrays]


def after_specs(after):
    return [SMEM if a.ndim == 1 else VMEM for a in after]


def after_args(after):
    return [a if a.ndim == 1 else vmem([a])[0] for a in after]


def params(mib):
    return pltpu.CompilerParams(vmem_limit_bytes=mib * 2**20)


def prefetch(grid, in_specs, out_specs, scratch=()):
    return pltpu.PrefetchScalarGridSpec(
        num_scalar_prefetch=1,
        grid=grid,
        in_specs=in_specs,
        out_specs=out_specs,
        scratch_shapes=scratch,
    )


def partial_kernel(n, count, tokens, grads, out, done, held, cotangents, masked, made, in_sems, out_sems):
    width = held.shape[2]

    def load(i):
        return pltpu.make_async_copy(tokens.at[:, pl.ds(i * width, width)], held.at[i], in_sems.at[i])

    def store(i):
        return pltpu.make_async_copy(made.at[i], out.at[pl.ds(i * width, width)], out_sems.at[i])

    load_grads = pltpu.make_async_copy(grads, cotangents, in_sems.at[n])
    load_grads.start()
    for i in range(n):
        load(i).start()
    load_grads.wait()
    live = lax.broadcasted_iota(jnp.int32, masked.shape, 0) < count[0]
    masked[...] = jnp.where(live, cotangents[...].astype(F32), 0.0).astype(BF)
    for i in range(n):
        load(i).wait()
        made[i] = jnp.dot(held[i].T, masked[...], preferred_element_type=F32).astype(BF)
        store(i).start()
    for i in range(n):
        store(i).wait()
    done[0] = 0


def partial_gradient(count, tokens, grads):
    cap, feats = tokens.shape
    ffw = grads.shape[1]
    n = 7
    return pl.pallas_call(
        functools.partial(partial_kernel, n),
        out_shape=[pltpu.HBM((feats, ffw), BF), jax.ShapeDtypeStruct((1,), jnp.int32)],
        grid_spec=prefetch(
            (1,),
            [ANY, ANY],
            [ANY, SMEM],
            [
                pltpu.VMEM((n, cap, feats // n), BF),
                pltpu.VMEM((cap, ffw), BF),
                pltpu.VMEM((cap, ffw), BF),
                pltpu.VMEM((n, feats // n, ffw), BF),
                pltpu.SemaphoreType.DMA((n + 1,)),
                pltpu.SemaphoreType.DMA((n,)),
            ],
        ),
        compiler_params=params(40),
    )(count, *hbm((tokens, grads)))


MY_X, MOVED, LEAVER, GO_UP, GO_DOWN, PICK = 0, 1, 2, 3, 4, 5
FAR_UP, FAR_DOWN, PICK_FAR = PICK + NX, PICK + NX + 1, PICK + NX + 2


def plan_kernel(place, new_owner, out):
    my_x, my_z = place[0], place[1]
    me = my_x * NZ + my_z
    leaver, moved, up, down = jnp.int32(0), jnp.int32(0), jnp.int32(0), jnp.int32(0)
    far_up, far_down = jnp.int32(0), jnp.int32(0)
    for e in range(N):
        to = new_owner[e]
        x, z = e // NZ, e % NZ
        away = (to + NZ - z) % NZ
        mine = (my_z == z) & (away != 0)
        dist = (x + NX - my_x) % NX
        leaver += jnp.where(mine, dist, 0)
        up += jnp.where(mine & (away <= UP), 1, 0)
        down += jnp.where(mine & (away > UP), 1, 0)
        moved += jnp.where((to == me) & (to != e), 1, 0)

        above, below = (z + 1) % NZ == my_z, (z + NZ - 1) % NZ == my_z
        far_up += jnp.where((my_z == z) & (away == 3), dist, 0)
        far_up += jnp.where(above & (away == 4), NX, 0) + jnp.where(below & (away == 2), NX + 1, 0)
        far_down += jnp.where((my_z == z) & (away == NZ - 3), dist, 0)
        far_down += jnp.where(above & (away == NZ - 2), NX, 0)

        @pl.when(to % NZ == my_z)
        def _():
            near = jnp.where(away == 1, NX, NX + 1)
            far = jnp.where(away <= UP, NX + 2, NX + 3)
            hop = jnp.where((away == 1) | (away == NZ - 1), near, far)
            out[PICK_FAR + (to // NZ + NX - my_x) % NX] = jnp.where(away == 0, dist, hop)
            along = jnp.where(away <= UP, NX - 1 + away, NX + UP + NZ - 1 - away)
            out[PICK + (to // NZ + NX - my_x) % NX] = jnp.where(away == 0, dist, along)

    out[MY_X] = my_x
    out[MOVED] = moved
    out[LEAVER] = leaver
    out[GO_UP] = up
    out[GO_DOWN] = down
    out[FAR_UP] = far_up
    out[FAR_DOWN] = far_down


def make_plan(place, new_owner):
    return pl.pallas_call(
        plan_kernel,
        out_shape=jax.ShapeDtypeStruct((PICK_FAR + NX,), jnp.int32),
        in_specs=[SMEM] * 2,
        out_specs=SMEM,
    )(place, new_owner)


def pack_kernel(n, place, *refs):
    own, outs, (held, sems) = refs[:n], refs[-2 - n * NX : -2], refs[-2:]
    part = outs[0].shape[0]

    def load(u, d):
        start = pl.multiple_of((place[0] + d) % NX * part, part)
        return pltpu.make_async_copy(
            own[u].at[pl.ds(start, part)],
            held.at[d] if own[u].dtype == F32 else outs[u * NX + d],
            sems.at[u, d],
        )

    for u in range(n):
        for d in range(NX):
            load(u, d).start()
    for u in range(n):
        for d in range(NX):
            load(u, d).wait()
            if own[u].dtype == F32:
                outs[u * NX + d][...] = held[d].astype(BF)


def pack(place, own, after=()):
    rows, width = own[0].shape
    part, n = rows // NX, len(own)
    made = pl.pallas_call(
        functools.partial(pack_kernel, n),
        out_shape=[pltpu.VMEM((part, width), BF)] * (NX * n),
        in_specs=[SMEM] + [ANY] * n + after_specs(after),
        out_specs=[VMEM] * (NX * n),
        scratch_shapes=[pltpu.VMEM((NX, part, width), F32), pltpu.SemaphoreType.DMA((n, NX))],
        compiler_params=params(16),
    )(place, *hbm(own), *after_args(after))
    return [made[u * NX : (u + 1) * NX] for u in range(n)]


def pick_kernel(n, which, n_out, plan, *refs):
    cases, outs, done = refs[:n], refs[-1 - n_out : -1], refs[-1]
    for out, chosen in zip(outs, which(plan)):
        for c in range(n):

            @pl.when(chosen == c)
            def _():
                out[...] = cases[c][...]

    done[0] = 0


def pick(plan, which, n_out, cases, after=()):
    shape = cases[0].shape
    return pl.pallas_call(
        functools.partial(pick_kernel, len(cases), which, n_out),
        out_shape=[pltpu.VMEM(shape, BF)] * n_out + [jax.ShapeDtypeStruct((1,), jnp.int32)],
        in_specs=[SMEM] + [VMEM] * len(cases) + after_specs(after),
        out_specs=[VMEM] * n_out + [SMEM],
        compiler_params=params(16),
    )(plan, *vmem(cases), *after_args(after))


def ring(a, axis, size, by):
    return lax.ppermute(a, axis, [(i, (i + by) % size) for i in range(size)])


def swap_x(pieces):
    came = list(pieces)
    for d in (1, 3, 2):
        came[(-d) % NX] = ring(pieces[d], "x", NX, d)
    return came


def along_z(plan, spreads):
    n = len(spreads)
    first, done = pick(plan, lambda plan: [plan[LEAVER]], 1, spreads[0])
    ups, downs = [ring(first, "z", NZ, 1)], [ring(first, "z", NZ, -1)]

    def own_or_passed(plan):
        return [
            jnp.where(plan[GO_UP] != 0, plan[LEAVER], NX),
            jnp.where(plan[GO_DOWN] != 0, plan[LEAVER], NX + 1),
        ]

    for t in range(1, n):
        up, down, done = pick(plan, own_or_passed, 2, [*spreads[t], ups[-1], downs[-1]])
        ups.append(ring(up, "z", NZ, 1))
        downs.append(ring(down, "z", NZ, -1))
    while len(ups) < n + UP - 1:
        ups.append(ring(ups[-1], "z", NZ, 1))
    while len(downs) < n + DOWN - 1:
        downs.append(ring(downs[-1], "z", NZ, -1))
    return [ups[j : j + UP] + downs[j : j + DOWN] for j in range(n)], done


def hop_near(plan, spread, after):
    first, done = pick(plan, lambda plan: [plan[LEAVER]], 1, spread, after)
    return [ring(first, "z", NZ, 1), ring(first, "z", NZ, -1)], done


def hop_far(plan, spread, near, after):
    up, down, done = pick(
        plan, lambda plan: [plan[FAR_UP], plan[FAR_DOWN]], 2, [*spread, *near], after
    )
    return [ring(up, "z", NZ, 3), ring(down, "z", NZ, -3)], done


def deliver(plan, at, spread, came, after=()):
    def delivered(plan):
        return [plan[at + d] for d in range(NX)]

    *pieces, done = pick(plan, delivered, NX, [*spread, *came], after)
    return swap_x(pieces), done


def adam_kernel(n, plan, own_master, own_one, own_two, *refs):
    grads, masters, ones, twos = (refs[k * n : (k + 1) * n] for k in range(4))
    out_master, out_one, out_two, out_weight = refs[-4:]
    step = pl.program_id(0)
    here = plan[MOVED] != 0

    def update(d, master, moment_one, moment_two):
        gradient = grads[d][...].astype(F32)
        param = master[...].astype(F32)
        moment_new = beta_one * moment_one[...].astype(F32) + (1.0 - beta_one) * gradient
        second_new = beta_two * moment_two[...].astype(F32) + (1.0 - beta_two) * gradient * gradient
        scaled_one = moment_new / (1.0 - beta_one**STEP)
        scaled_two = second_new / (1.0 - beta_two**STEP)
        updated = param - learn_rate * (
            scaled_one / (jnp.sqrt(scaled_two) + adam_eps) + decay_rate * param
        )
        out_master[...] = updated
        out_one[...] = moment_new.astype(BF)
        out_two[...] = second_new.astype(BF)
        out_weight[...] = updated.astype(BF)

    for d in range(n):

        @pl.when(here & (step == d))
        def _():
            update(d, masters[d], ones[d], twos[d])

        @pl.when(jnp.logical_not(here) & (step == d))
        def _():
            update(d, own_master, own_one, own_two)


def adam(plan, first, n, grads, own, came, before=(), after=()):
    rows, width = own[0].shape
    part = rows // NX
    spec = pl.BlockSpec((part, width), lambda i, plan: ((plan[MY_X] + first + i) % NX, 0))
    moved = [a for unit in (grads, *came) for a in unit[first : first + n]]
    return pl.pallas_call(
        functools.partial(adam_kernel, n),
        out_shape=[jax.ShapeDtypeStruct((rows, width), d) for d in (F32, BF, BF, BF)],
        grid_spec=prefetch(
            (n,), [spec] * 3 + [VMEM] * len(moved) + [ANY] * len(before) + after_specs(after), [spec] * 4
        ),
        input_output_aliases={4 + len(moved) + k: k for k in range(len(before))},
        compiler_params=params(24),
    )(plan, *hbm(own), *vmem(moved), *before, *after_args(after))


def local(tokens_in, grad_out, token_counts, new_owner, master, moment_one, moment_two):
    place = jnp.stack([lax.axis_index("x"), lax.axis_index("z")]).astype(jnp.int32)
    own = (master[0], moment_one[0], moment_two[0])
    partial, made = partial_gradient(token_counts[0], tokens_in[0], grad_out[0])
    summed = lax.psum_scatter(partial, ("y", "core"), scatter_dimension=0, tiled=True)
    plan = make_plan(place, new_owner)

    packed = pack(place, own[1:2], [made]) + pack(place, [own[2], own[0]], [plan])
    spreads = [swap_x(pieces) for pieces in packed]
    rows, _ = along_z(plan, spreads)
    grad_spread = swap_x(pack(place, [summed], [rows[2][0], rows[2][UP]])[0])
    came_0, done = deliver(plan, PICK, spreads[0], rows[0])
    near, done = hop_near(plan, grad_spread, [done])
    came_1, done = deliver(plan, PICK, spreads[1], rows[1], [done])
    far, done = hop_far(plan, grad_spread, near, [done])
    ahead = [*came_0[1:], came_1[1], came_1[3]]
    came_2, _ = deliver(plan, PICK, spreads[2], rows[2], [done, *ahead])
    ahead = [*came_0[1:], *came_1[1:]]
    gradient, _ = deliver(plan, PICK_FAR, grad_spread, near + far, ahead)
    came = (came_2, came_0, came_1)
    outs = adam(plan, 0, 2, gradient, own, came, after=came_2[2:])
    outs = adam(plan, 2, 2, gradient, own, came, outs)
    return tuple(o[None] for o in outs)


def solution(mesh):
    n_dp = mesh.devices.shape[0]
    fine = Mesh(mesh.devices.reshape(n_dp // 2, 2, NX, NZ), ("y", "core", "x", "z"))
    dp, expert = ("y", "core"), ("x", "z")
    whole = P(expert, dp, None)
    return jax.shard_map(
        local,
        mesh=fine,
        in_specs=(whole, whole, P(expert, dp), P(), whole, whole, whole),
        out_specs=(whole, whole, whole, whole),
        check_vma=False,
    )
```
